32 devices in a mesh: row: 4 (over y, x), col: 8 (over z, core).
Axes of the slice: x: 2, y: 2, z: 4, core: 2. Of those that a mesh axis runs over, the one named last changes fastest.
Arguments:
- tokens: bfloat16 [512, 8192], P('col', 'row'), may hold values from -6 to 6
- cotangent: bfloat16 [512, 8192], P('col', 'row'), may hold values from -6 to 6
- gate_weight: bfloat16 [8192, 32768], P('row', 'col'), may hold values from -0.125 to 0.125
- up_weight: bfloat16 [8192, 32768], P('row', 'col'), may hold values from -0.125 to 0.125
- down_weight: bfloat16 [32768, 8192], P('col', 'row'), may hold values from -0.0625 to 0.0625
- block_mask: int32 [3, 16, 64], P(None, 'row', 'col'), may hold values 0 or 1
Outputs:
- input_grad: bfloat16 [512, 8192], P('col', 'row')
- gate_grad: bfloat16 [8192, 32768], P('row', 'col')
- up_grad: bfloat16 [8192, 32768], P('row', 'col')
- down_grad: bfloat16 [32768, 8192], P('col', 'row')
The draws below stay inside these ranges and needn't reach their ends.
All inputs are finite; a program needn't handle non-finite values. No bound on the sum of `block_mask` on one device may be relied on, other than what follows from the above.
Results may differ from the reference program's by a relative error of at most 0.005.
Values may be sent and summed in bfloat16 or wider, within the bound.
A program may use at most 256 MiB of HBM per device.

```python
import jax
import jax.numpy as jnp

D = 8192
FF = 32768
BLK = 512
TOKENS = 512
DB = 16
FB = 64


def place_ends(array, key, low, high):
    place = [jax.random.randint(jax.random.fold_in(key, axis), (), 0, length) for axis, length in enumerate(array.shape)]
    widest = array.shape.index(max(array.shape))
    beside = place[:widest] + [(place[widest] + 1) % array.shape[widest]] + place[widest + 1:]
    return array.at[tuple(place)].set(low).at[tuple(beside)].set(high)


def shard_levels(own_key, shape, shards, least, top_value):
    factor_of, own = 1.0, jax.random.fold_in(own_key, 6)
    for position, shards_of in shards:
        draws = jnp.exp(jax.random.uniform(jax.random.fold_in(own, position), (shards_of,), jnp.float32, least / len(shards), top_value / len(shards)))
        factor_of = factor_of * jnp.repeat(draws, shape[position] // shards_of).reshape([-1 if axis == position else 1 for axis in range(len(shape))])
    return factor_of


def normal_values(stream_key, dims, spread, reach, cuts=(), kind=jnp.bfloat16):
    result = jax.random.normal(stream_key, dims, jnp.float32) * spread
    if len(cuts) > 0:
        result = shard_levels(stream_key, dims, cuts, -0.22, 0.18) * result
    return jnp.clip(result, min=-reach, max=reach).astype(kind)


def setup_inputs(seed: int = 0) -> dict:
    arg_keys = jax.random.split(jax.random.key(seed), 7)
    tokens = normal_values(arg_keys[0], (TOKENS, D), 1.0, 6.0, ((0, 8), (1, 4)))
    cotangent = normal_values(arg_keys[1], (TOKENS, D), 1.0, 6.0, ((0, 8), (1, 4)))
    gate_weight = normal_values(arg_keys[2], (D, FF), (D // 4) ** -0.5, 0.125, ((0, 4), (1, 8)))
    up_weight = normal_values(arg_keys[3], (D, FF), (D // 4) ** -0.5, 0.125, ((0, 4), (1, 8)))
    down_weight = normal_values(arg_keys[4], (FF, D), (FF // 4) ** -0.5, 0.0625, ((0, 8), (1, 4)))
    block_mask = place_ends((jax.random.randint(arg_keys[5], (3, DB, FB), 0, 4) < 1).astype(jnp.int32), jax.random.fold_in(arg_keys[5], 1), 0, 1)
    return dict(tokens=tokens, cotangent=cotangent, gate_weight=gate_weight, up_weight=up_weight, down_weight=down_weight, block_mask=block_mask)


def expand(kept_map):
    return jnp.repeat(jnp.repeat(kept_map, BLK, axis=0), BLK, axis=1).astype(jnp.bfloat16)


def reference(tokens, cotangent, gate_weight, up_weight, down_weight, block_mask):
    mask_gate = expand(block_mask[0])
    mask_up = expand(block_mask[1])
    mask_down = expand(block_mask[2]).T
    kept_gate = gate_weight * mask_gate
    kept_up = up_weight * mask_up
    kept_down = down_weight * mask_down
    gate_value = jnp.dot(tokens, kept_gate, preferred_element_type=jnp.float32)
    up_value = jnp.dot(tokens, kept_up, preferred_element_type=jnp.float32)
    hidden_grad = jnp.dot(cotangent, kept_down.T, preferred_element_type=jnp.float32)
    sigmoid = jax.nn.sigmoid(gate_value)
    swish = gate_value * sigmoid
    hidden = (swish * up_value).astype(jnp.bfloat16)
    gate_delta = (hidden_grad * up_value * sigmoid * (1.0 + gate_value * (1.0 - sigmoid))).astype(jnp.bfloat16)
    up_delta = (hidden_grad * swish).astype(jnp.bfloat16)
    down_grad = (jnp.dot(hidden.T, cotangent, preferred_element_type=jnp.float32) * mask_down).astype(jnp.bfloat16)
    gate_grad = (jnp.dot(tokens.T, gate_delta, preferred_element_type=jnp.float32) * mask_gate).astype(jnp.bfloat16)
    up_grad = (jnp.dot(tokens.T, up_delta, preferred_element_type=jnp.float32) * mask_up).astype(jnp.bfloat16)
    input_grad = (jnp.dot(gate_delta, kept_gate.T, preferred_element_type=jnp.float32)
                  + jnp.dot(up_delta, kept_up.T, preferred_element_type=jnp.float32)).astype(jnp.bfloat16)
    return (input_grad, gate_grad, up_grad, down_grad)
```

```python
import functools

import jax
import jax.numpy as jnp
from jax import lax
from jax.experimental import pallas as pl
from jax.experimental.pallas import tpu as pltpu
from jax.sharding import PartitionSpec as P

BLK = 512
VMEM_LIMIT = 40 * 1024 * 1024

NN = (((1,), (0,)), ((), ()))
NT = (((1,), (1,)), ((), ()))
TN = (((0,), (0,)), ((), ()))


def dot(a, b, dims):
    return lax.dot_general(a, b, dims, preferred_element_type=jnp.float32)


def forward_kernel(flags, *refs, kinds):
    count = len(kinds)
    acts, weights = refs[:count], refs[count : 2 * count]
    keep, give, acc = refs[2 * count :]
    step = pl.program_id(0)
    steps = pl.num_programs(0)

    @pl.when(step == 0)
    def _():
        acc[...] = jnp.zeros_like(acc)

    for i, kind in enumerate(kinds):

        @pl.when(flags[1 + kind * steps + step] != 0)
        def _(i=i, kind=kind):
            dims = NT if kind == 2 else NN
            acc[i] += dot(acts[i][...], weights[i][...], dims)

    @pl.when(step == steps - 1)
    def _():
        half = acc.shape[1] // 2
        mine = pl.multiple_of(flags[0] * half, half)
        other = pl.multiple_of((1 - flags[0]) * half, half)
        for i in range(count):
            keep[i] = acc[i, pl.ds(mine, half), :]
            give[i] = acc[i, pl.ds(other, half), :].astype(give.dtype)


def forward(flags, acts, weights, kinds, block, wire):
    tokens, width = acts[0].shape
    steps = width // BLK
    count = len(kinds)
    half = (count, tokens // 2, BLK)
    weight_specs = [
        pl.BlockSpec((BLK, BLK), (lambda d, f: (block, d)) if kind == 2 else (lambda d, f: (d, block)))
        for kind in kinds
    ]
    return pl.pallas_call(
        functools.partial(forward_kernel, kinds=kinds),
        grid_spec=pltpu.PrefetchScalarGridSpec(
            num_scalar_prefetch=1,
            grid=(steps,),
            in_specs=[pl.BlockSpec((tokens, BLK), lambda d, f: (0, d))] * count + weight_specs,
            out_specs=[pl.BlockSpec(half, lambda d, f: (0, 0, 0))] * 2,
            scratch_shapes=[pltpu.VMEM((count, tokens, BLK), jnp.float32)],
        ),
        out_shape=[jax.ShapeDtypeStruct(half, jnp.float32), jax.ShapeDtypeStruct(half, wire)],
        compiler_params=pltpu.CompilerParams(vmem_limit_bytes=VMEM_LIMIT),
        cost_estimate=pl.CostEstimate(
            flops=2 * count * tokens * width * BLK,
            bytes_accessed=count * (2 * width * (tokens + BLK) + 3 * tokens * BLK),
            transcendentals=0,
        ),
        name="forward_part",
    )(flags, *acts, *weights)


def backward_kernel(flags, deltas, tokens, cotan, gate, up, *refs, first):
    acc_in = None if first else refs[0]
    acc, gate_grad, up_grad, down_grad = refs[0 if first else 4 :]
    step = pl.program_id(0)
    steps = pl.num_programs(0)
    total = jnp.zeros(acc.shape, jnp.float32) if first else acc_in[...]
    acc[...] = total

    def kept(kind):
        return flags[1 + kind * steps + step] != 0

    for kind, weight, grad in ((0, gate, gate_grad), (1, up, up_grad)):

        @pl.when(kept(kind))
        def _(kind=kind, weight=weight, grad=grad):
            delta = deltas[kind]
            acc[...] += dot(delta, weight[...], NT)
            grad[...] = dot(tokens[...], delta, TN).astype(grad.dtype)

        @pl.when(jnp.logical_not(kept(kind)))
        def _(grad=grad):
            grad[...] = jnp.zeros_like(grad)

    @pl.when(kept(2))
    def _():
        down_grad[...] = dot(deltas[2], cotan[...], TN).astype(down_grad.dtype)

    @pl.when(jnp.logical_not(kept(2)))
    def _():
        down_grad[...] = jnp.zeros_like(down_grad)


def backward(flags, deltas, tokens_all, cotan_all, gate_weight, up_weight, sums, block):
    tokens, width = tokens_all.shape
    hidden = gate_weight.shape[1]
    first = sums is None
    act_spec = pl.BlockSpec((tokens, BLK), lambda d, f: (0, d))
    weight_spec = pl.BlockSpec((BLK, BLK), lambda d, f: (d, block))
    down_spec = pl.BlockSpec((BLK, BLK), lambda d, f: (block, d))
    any_spec = pl.BlockSpec(memory_space=pl.ANY)
    in_specs = [
        pl.BlockSpec((3, tokens, BLK), lambda d, f: (0, 0, 0)),
        act_spec,
        act_spec,
        weight_spec,
        weight_spec,
    ]
    operands = [deltas, tokens_all, cotan_all, gate_weight, up_weight]
    aliases = {}
    if not first:
        in_specs += [act_spec, any_spec, any_spec, any_spec]
        operands += list(sums)
        aliases = {6: 0, 7: 1, 8: 2, 9: 3}
    return pl.pallas_call(
        functools.partial(backward_kernel, first=first),
        grid_spec=pltpu.PrefetchScalarGridSpec(
            num_scalar_prefetch=1,
            grid=(width // BLK,),
            in_specs=in_specs,
            out_specs=[act_spec, weight_spec, weight_spec, down_spec],
        ),
        out_shape=[
            jax.ShapeDtypeStruct((tokens, width), jnp.float32),
            jax.ShapeDtypeStruct((width, hidden), jnp.bfloat16),
            jax.ShapeDtypeStruct((width, hidden), jnp.bfloat16),
            jax.ShapeDtypeStruct((hidden, width), jnp.bfloat16),
        ],
        input_output_aliases=aliases,
        compiler_params=pltpu.CompilerParams(vmem_limit_bytes=VMEM_LIMIT),
        cost_estimate=pl.CostEstimate(
            flops=10 * tokens * width * BLK,
            bytes_accessed=10 * width * BLK + 12 * tokens * width,
            transcendentals=0,
        ),
        name="backward_part",
    )(flags, *operands)


def swiglu(gate_value, up_value, hidden_grad):
    sigmoid = jax.nn.sigmoid(gate_value)
    swish = gate_value * sigmoid
    hidden = swish * up_value
    gate_delta = hidden_grad * up_value * sigmoid * (1.0 + gate_value * (1.0 - sigmoid))
    up_delta = hidden_grad * swish
    return jnp.stack([gate_delta, up_delta, hidden]).astype(jnp.bfloat16)


def shards(tokens, cotangent, gate_weight, up_weight, down_weight, block_mask):
    rows = lax.axis_size("row")
    levels = rows.bit_length() - 1
    row = lax.axis_index("row")
    wire = jnp.bfloat16 if rows <= 4 else jnp.float32
    blocks = gate_weight.shape[1] // BLK

    def swap(part, bit):
        return lax.ppermute(part, "row", [(i, i ^ (1 << bit)) for i in range(rows)])

    def side(bit):
        return (row >> bit) & 1

    def finish_sum(keep, give, order):
        part = keep + swap(give, order[0]).astype(jnp.float32)
        for bit in order[1:]:
            half = part.shape[1] // 2
            mine = lax.dynamic_slice_in_dim(part, side(bit) * half, half, 1)
            other = lax.dynamic_slice_in_dim(part, (1 - side(bit)) * half, half, 1)
            part = mine + swap(other.astype(wire), bit).astype(jnp.float32)
        return part

    def spread(part, order):
        for bit in reversed(order):
            got = swap(part, bit)
            low = jnp.where(side(bit) == 0, part, got)
            high = jnp.where(side(bit) == 0, got, part)
            part = jnp.concatenate([low, high], axis=1)
        return part

    orders = [
        tuple(range(levels)) if block % 2 == 0 else tuple(reversed(range(levels)))
        for block in range(blocks)
    ]
    flags = [
        jnp.concatenate(
            [side(order[0]).reshape(1).astype(jnp.int32), block_mask[:, :, block].reshape(-1)]
        )
        for block, order in enumerate(orders)
    ]

    tokens_all = lax.all_gather(tokens, "col", axis=0, tiled=True)
    cotan_all = lax.all_gather(cotangent, "col", axis=0, tiled=True)

    values = [
        forward(flags[b], [tokens_all] * 2, [gate_weight, up_weight], (0, 1), b, wire)
        for b in range(blocks)
    ]
    grads = [forward(flags[b], [cotan_all], [down_weight], (2,), b, wire) for b in range(blocks)]
    sums = None
    for b in range(blocks):
        pair = finish_sum(*values[b], orders[b])
        grad = finish_sum(*grads[b], orders[b])
        deltas = spread(swiglu(pair[0], pair[1], grad[0]), orders[b])
        sums = backward(
            flags[b], deltas, tokens_all, cotan_all, gate_weight, up_weight, sums, b
        )
    total, gate_grad, up_grad, down_grad = sums
    input_grad = lax.psum_scatter(total, "col", scatter_dimension=0, tiled=True)
    return (input_grad.astype(jnp.bfloat16), gate_grad, up_grad, down_grad)


def solution(mesh):
    in_specs = (
        P("col", "row"),
        P("col", "row"),
        P("row", "col"),
        P("row", "col"),
        P("col", "row"),
        P(None, "row", "col"),
    )
    out_specs = (P("col", "row"), P("row", "col"), P("row", "col"), P("col", "row"))
    return jax.shard_map(shards, mesh=mesh, in_specs=in_specs, out_specs=out_specs, check_vma=False)
```

```python
import functools

import jax
import jax.numpy as jnp
from jax import lax
from jax.experimental import pallas as pl
from jax.experimental.pallas import tpu as pltpu
from jax.sharding import PartitionSpec as P

BLK = 512
VMEM_LIMIT = 40 * 1024 * 1024

NN = (((1,), (0,)), ((), ()))
NT = (((1,), (1,)), ((), ()))
TN = (((0,), (0,)), ((), ()))


def dot(a, b, dims):
    return lax.dot_general(a, b, dims, preferred_element_type=jnp.float32)


def forward_kernel(flags, acts, *refs, kinds):
    count = len(kinds)
    weights = refs[:count]
    keep, give, acc = refs[count:]
    inner, step = pl.program_id(0), pl.program_id(1)
    group, steps = pl.num_programs(0), pl.num_programs(1)

    @pl.when(step == 0)
    def _():
        acc[...] = jnp.zeros_like(acc)

    for i, kind in enumerate(kinds):

        @pl.when(flags[1 + (kind * steps + step) * group + inner] != 0)
        def _(i=i, kind=kind):
            acc[i] += dot(acts[...], weights[i][...], NT if kind == 2 else NN)

    @pl.when(step == steps - 1)
    def _():
        half = acc.shape[1] // 2
        mine = pl.multiple_of(flags[0] * half, half)
        other = pl.multiple_of((1 - flags[0]) * half, half)
        for i in range(count):
            keep[i] = acc[i, pl.ds(mine, half), :]
            give[i] = acc[i, pl.ds(other, half), :].astype(give.dtype)


def forward(flags, acts, weights, kinds, start, group, wire):
    tokens, width = acts.shape
    steps = width // BLK
    count = len(kinds)
    half = (count, tokens // 2, group * BLK)
    weight_specs = [
        pl.BlockSpec(
            (BLK, BLK),
            (lambda j, d, f: (start + j, d)) if kind == 2 else (lambda j, d, f: (d, start + j)),
        )
        for kind in kinds
    ]
    return pl.pallas_call(
        functools.partial(forward_kernel, kinds=kinds),
        grid_spec=pltpu.PrefetchScalarGridSpec(
            num_scalar_prefetch=1,
            grid=(group, steps),
            in_specs=[pl.BlockSpec((tokens, BLK), lambda j, d, f: (0, d))] + weight_specs,
            out_specs=[pl.BlockSpec((count, tokens // 2, BLK), lambda j, d, f: (0, 0, j))] * 2,
            scratch_shapes=[pltpu.VMEM((count, tokens, BLK), jnp.float32)],
        ),
        out_shape=[jax.ShapeDtypeStruct(half, jnp.float32), jax.ShapeDtypeStruct(half, wire)],
        compiler_params=pltpu.CompilerParams(vmem_limit_bytes=VMEM_LIMIT),
        cost_estimate=pl.CostEstimate(
            flops=2 * count * tokens * width * BLK * group,
            bytes_accessed=group * (count * (2 * width * BLK + 3 * tokens * BLK) + 2 * width * tokens),
            transcendentals=0,
        ),
        name="forward_part",
    )(flags, acts, *weights)


def input_kernel(flags, near, far, gate, up, *refs):
    acc = refs[-1]
    step, inner = pl.program_id(0), pl.program_id(1)
    steps, group = pl.num_programs(0), pl.num_programs(1)

    @pl.when(inner == 0)
    def _():
        acc[...] = refs[0][...] if len(refs) == 2 else jnp.zeros_like(acc)

    half = near.shape[1]
    for kind, weight in ((0, gate), (1, up)):

        @pl.when(flags[1 + (kind * steps + step) * group + inner] != 0)
        def _(kind=kind, weight=weight):
            for delta, place in ((near, flags[0]), (far, 1 - flags[0])):
                rows = pl.ds(pl.multiple_of(place * half, half), half)
                acc[rows, :] += dot(delta[kind], weight[...], NT)


def add_input_grad(flags, near, far, gate_weight, up_weight, total, start, group):
    half = near.shape[1]
    tokens, width = 2 * half, gate_weight.shape[0]
    delta_spec = pl.BlockSpec((2, half, BLK), lambda d, j, f: (0, 0, j))
    weight_spec = pl.BlockSpec((BLK, BLK), lambda d, j, f: (d, start + j))
    acc_spec = pl.BlockSpec((tokens, BLK), lambda d, j, f: (0, d))
    first = total is None
    return pl.pallas_call(
        input_kernel,
        grid_spec=pltpu.PrefetchScalarGridSpec(
            num_scalar_prefetch=1,
            grid=(width // BLK, group),
            in_specs=[delta_spec] * 2 + [weight_spec] * 2 + ([] if first else [acc_spec]),
            out_specs=acc_spec,
        ),
        out_shape=jax.ShapeDtypeStruct((tokens, width), jnp.float32),
        input_output_aliases={} if first else {5: 0},
        compiler_params=pltpu.CompilerParams(vmem_limit_bytes=VMEM_LIMIT),
        cost_estimate=pl.CostEstimate(
            flops=4 * tokens * width * BLK * group,
            bytes_accessed=4 * width * BLK * group + 8 * tokens * width,
            transcendentals=0,
        ),
        name="input_grad_part",
    )(flags, near, far, gate_weight, up_weight, *([] if first else [total]))


def weight_kernel(flags, near, far, tokens, cotan, *refs):
    grads = refs[-3:]
    step, inner = pl.program_id(0), pl.program_id(1)
    steps, group = pl.num_programs(0), pl.num_programs(1)
    half = near.shape[1]
    columns = pl.ds(pl.multiple_of(inner * BLK, BLK), BLK)
    mine = pl.ds(pl.multiple_of(flags[0] * half, half), half)
    other = pl.ds(pl.multiple_of((1 - flags[0]) * half, half), half)
    for kind, grad in enumerate(grads):
        kept = flags[1 + (kind * steps + step) * group + inner] != 0

        @pl.when(kept)
        def _(kind=kind, grad=grad):
            one, two = near[kind, :, columns], far[kind, :, columns]
            if kind == 2:
                value = dot(one, cotan[mine, :], TN) + dot(two, cotan[other, :], TN)
            else:
                value = dot(tokens[mine, :], one, TN) + dot(tokens[other, :], two, TN)
            grad[...] = value.astype(grad.dtype)

        @pl.when(jnp.logical_not(kept))
        def _(grad=grad):
            grad[...] = jnp.zeros_like(grad)


def weight_grads(flags, near, far, tokens_all, cotan_all, grads, hidden, start, group):
    tokens, width = tokens_all.shape
    act_spec = pl.BlockSpec((tokens, BLK), lambda d, j, f: (0, d))
    delta_spec = pl.BlockSpec(near.shape, lambda d, j, f: (0, 0, 0))
    grad_spec = pl.BlockSpec((BLK, BLK), lambda d, j, f: (d, start + j))
    down_spec = pl.BlockSpec((BLK, BLK), lambda d, j, f: (start + j, d))
    any_spec = pl.BlockSpec(memory_space=pl.ANY)
    first = grads is None
    return pl.pallas_call(
        weight_kernel,
        grid_spec=pltpu.PrefetchScalarGridSpec(
            num_scalar_prefetch=1,
            grid=(width // BLK, group),
            in_specs=[delta_spec] * 2 + [act_spec] * 2 + ([] if first else [any_spec] * 3),
            out_specs=[grad_spec, grad_spec, down_spec],
        ),
        out_shape=[
            jax.ShapeDtypeStruct((width, hidden), jnp.bfloat16),
            jax.ShapeDtypeStruct((width, hidden), jnp.bfloat16),
            jax.ShapeDtypeStruct((hidden, width), jnp.bfloat16),
        ],
        input_output_aliases={} if first else {5: 0, 6: 1, 7: 2},
        compiler_params=pltpu.CompilerParams(vmem_limit_bytes=VMEM_LIMIT),
        cost_estimate=pl.CostEstimate(
            flops=6 * tokens * width * BLK * group,
            bytes_accessed=6 * width * BLK * group + 4 * tokens * width,
            transcendentals=0,
        ),
        name="weight_grad_part",
    )(flags, near, far, tokens_all, cotan_all, *([] if first else grads))


def swiglu(gate_value, up_value, hidden_grad):
    sigmoid = jax.nn.sigmoid(gate_value)
    swish = gate_value * sigmoid
    hidden = swish * up_value
    gate_delta = hidden_grad * up_value * sigmoid * (1.0 + gate_value * (1.0 - sigmoid))
    up_delta = hidden_grad * swish
    return jnp.stack([gate_delta, up_delta, hidden]).astype(jnp.bfloat16)


def shards(tokens, cotangent, gate_weight, up_weight, down_weight, block_mask):
    rows = lax.axis_size("row")
    levels = rows.bit_length() - 1
    row = lax.axis_index("row")
    wire = jnp.bfloat16 if rows <= 4 else jnp.float32
    hidden = gate_weight.shape[1]
    blocks = hidden // BLK
    group = 2 if blocks % 2 == 0 else 1
    groups = blocks // group

    def swap(part, bit):
        return lax.ppermute(part, "row", [(i, i ^ (1 << bit)) for i in range(rows)])

    def side(bit):
        return (row >> bit) & 1

    def after(value, earlier):
        return lax.optimization_barrier((value, earlier))

    def finish_sum(value, slope, order):
        got = swap(value[1], order[0])
        give, got = after(slope[1], got)
        parts = [
            value[0] + got.astype(jnp.float32),
            slope[0] + swap(give, order[0]).astype(jnp.float32),
        ]
        for bit in order[1:]:
            half = parts[0].shape[1] // 2
            mine = [lax.dynamic_slice_in_dim(p, side(bit) * half, half, 1) for p in parts]
            other = [lax.dynamic_slice_in_dim(p, (1 - side(bit)) * half, half, 1) for p in parts]
            got = swap(jnp.concatenate([p.astype(wire) for p in other]), bit)
            parts = [
                mine[0] + got[: mine[0].shape[0]].astype(jnp.float32),
                mine[1] + got[mine[0].shape[0] :].astype(jnp.float32),
            ]
        return parts

    def spread(part, order):
        for bit in reversed(order[1:]):
            got = swap(part, bit)
            low = jnp.where(side(bit) == 0, part, got)
            high = jnp.where(side(bit) == 0, got, part)
            part = jnp.concatenate([low, high], axis=1)
        return part, swap(part, order[0])

    orders = [
        tuple(range(levels)) if g % 2 == 0 else tuple(reversed(range(levels)))
        for g in range(groups)
    ]
    flags = [
        jnp.concatenate(
            [
                side(order[0]).reshape(1).astype(jnp.int32),
                block_mask[:, :, g * group : (g + 1) * group].reshape(-1),
            ]
        )
        for g, order in enumerate(orders)
    ]

    tokens_all = lax.all_gather(tokens, "col", axis=0, tiled=True)
    cotan_all = lax.all_gather(cotangent, "col", axis=0, tiled=True)

    values, slopes, last = [], [], None
    for acts, weights, kinds, results in (
        (tokens_all, [gate_weight, up_weight], (0, 1), values),
        (cotan_all, [down_weight], (2,), slopes),
    ):
        for g in range(groups):
            order_flags = flags[g]
            if last is not None:
                order_flags, last[0] = after(order_flags, last[0])
            last = list(forward(order_flags, acts, weights, kinds, g * group, group, wire))
            results.append(last)
    total, halves = None, []
    for g in range(groups):
        pair, slope = finish_sum(values[g], slopes[g], orders[g])
        near, far = spread(swiglu(pair[0], pair[1], slope[0]), orders[g])
        halves.append((near, far))
        total = add_input_grad(
            flags[g], near, far, gate_weight, up_weight, total, g * group, group
        )
    input_grad = lax.psum_scatter(total, "col", scatter_dimension=0, tiled=True)
    grads = None
    for g, (near, far) in enumerate(halves):
        grads = weight_grads(
            flags[g], near, far, tokens_all, cotan_all, grads, hidden, g * group, group
        )
    return (input_grad.astype(jnp.bfloat16), *grads)


def solution(mesh):
    in_specs = (
        P("col", "row"),
        P("col", "row"),
        P("row", "col"),
        P("row", "col"),
        P("col", "row"),
        P(None, "row", "col"),
    )
    out_specs = (P("col", "row"), P("row", "col"), P("row", "col"), P("col", "row"))
    return jax.shard_map(shards, mesh=mesh, in_specs=in_specs, out_specs=out_specs, check_vma=False)
```

```python
import functools

import jax
import jax.numpy as jnp
from jax import lax
from jax.experimental import pallas as pl
from jax.experimental.pallas import tpu as pltpu
from jax.sharding import PartitionSpec as P

BLK = 512
VMEM_LIMIT = 40 * 1024 * 1024

NN = (((1,), (0,)), ((), ()))
NT = (((1,), (1,)), ((), ()))
TN = (((0,), (0,)), ((), ()))


def dot(a, b, dims):
    return lax.dot_general(a, b, dims, preferred_element_type=jnp.float32)


def forward_kernel(flags, acts, *refs, kinds):
    count = len(kinds)
    weights = refs[:count]
    keep, give, acc = refs[count:]
    inner, step = pl.program_id(0), pl.program_id(1)
    group, steps = pl.num_programs(0), pl.num_programs(1)

    @pl.when(step == 0)
    def _():
        acc[...] = jnp.zeros_like(acc)

    for i, kind in enumerate(kinds):

        @pl.when(flags[1 + (kind * steps + step) * group + inner] != 0)
        def _(i=i, kind=kind):
            acc[i] += dot(acts[...], weights[i][...], NT if kind == 2 else NN)

    @pl.when(step == steps - 1)
    def _():
        half = acc.shape[1] // 2
        mine = pl.multiple_of(flags[0] * half, half)
        other = pl.multiple_of((1 - flags[0]) * half, half)
        for i in range(count):
            keep[i] = acc[i, pl.ds(mine, half), :]
            give[i] = acc[i, pl.ds(other, half), :].astype(give.dtype)


def forward(flags, acts, weights, kinds, start, group, wire):
    tokens, width = acts.shape
    steps = width // BLK
    count = len(kinds)
    half = (count, tokens // 2, group * BLK)
    weight_specs = [
        pl.BlockSpec(
            (BLK, BLK),
            (lambda j, d, f: (start + j, d)) if kind == 2 else (lambda j, d, f: (d, start + j)),
        )
        for kind in kinds
    ]
    return pl.pallas_call(
        functools.partial(forward_kernel, kinds=kinds),
        grid_spec=pltpu.PrefetchScalarGridSpec(
            num_scalar_prefetch=1,
            grid=(group, steps),
            in_specs=[pl.BlockSpec((tokens, BLK), lambda j, d, f: (0, d))] + weight_specs,
            out_specs=[pl.BlockSpec((count, tokens // 2, BLK), lambda j, d, f: (0, 0, j))] * 2,
            scratch_shapes=[pltpu.VMEM((count, tokens, BLK), jnp.float32)],
        ),
        out_shape=[jax.ShapeDtypeStruct(half, jnp.float32), jax.ShapeDtypeStruct(half, wire)],
        compiler_params=pltpu.CompilerParams(vmem_limit_bytes=VMEM_LIMIT),
        cost_estimate=pl.CostEstimate(
            flops=2 * count * tokens * width * BLK * group,
            bytes_accessed=group * (count * (2 * width * BLK + 3 * tokens * BLK) + 2 * width * tokens),
            transcendentals=0,
        ),
        name="forward_part",
    )(flags, acts, *weights)


def input_kernel(flags, delta, gate, up, acc_in, acc):
    step, inner = pl.program_id(0), pl.program_id(1)
    steps, group = pl.num_programs(0), pl.num_programs(1)

    @pl.when(inner == 0)
    def _():
        acc[...] = acc_in[...]

    for kind, weight in ((0, gate), (1, up)):

        @pl.when(flags[1 + (kind * steps + step) * group + inner] != 0)
        def _(kind=kind, weight=weight):
            acc[...] += dot(delta[kind], weight[...], NT)


def add_input_grad(flags, delta, near, gate_weight, up_weight, total, start, group):
    half = delta.shape[1]
    tokens, width = total.shape
    delta_spec = pl.BlockSpec((2, half, BLK), lambda d, j, f: (0, 0, j))
    weight_spec = pl.BlockSpec((BLK, BLK), lambda d, j, f: (d, start + j))
    acc_spec = pl.BlockSpec((half, BLK), lambda d, j, f: (f[0] if near else 1 - f[0], d))
    return pl.pallas_call(
        input_kernel,
        grid_spec=pltpu.PrefetchScalarGridSpec(
            num_scalar_prefetch=1,
            grid=(width // BLK, group),
            in_specs=[delta_spec] + [weight_spec] * 2 + [acc_spec],
            out_specs=acc_spec,
        ),
        out_shape=jax.ShapeDtypeStruct((tokens, width), jnp.float32),
        input_output_aliases={4: 0},
        compiler_params=pltpu.CompilerParams(vmem_limit_bytes=VMEM_LIMIT),
        cost_estimate=pl.CostEstimate(
            flops=4 * half * width * BLK * group,
            bytes_accessed=4 * width * BLK * group + 8 * half * width,
            transcendentals=0,
        ),
        name="input_grad_part",
    )(flags, delta, gate_weight, up_weight, total)


def weight_kernel(flags, near, far, tokens, cotan, *refs):
    grads = refs[-3:]
    step, inner = pl.program_id(0), pl.program_id(1)
    steps, group = pl.num_programs(0), pl.num_programs(1)
    half = near.shape[1]
    columns = pl.ds(pl.multiple_of(inner * BLK, BLK), BLK)
    mine = pl.ds(pl.multiple_of(flags[0] * half, half), half)
    other = pl.ds(pl.multiple_of((1 - flags[0]) * half, half), half)
    for kind, grad in enumerate(grads):
        kept = flags[1 + (kind * steps + step) * group + inner] != 0

        @pl.when(kept)
        def _(kind=kind, grad=grad):
            one, two = near[kind, :, columns], far[kind, :, columns]
            if kind == 2:
                value = dot(one, cotan[mine, :], TN) + dot(two, cotan[other, :], TN)
            else:
                value = dot(tokens[mine, :], one, TN) + dot(tokens[other, :], two, TN)
            grad[...] = value.astype(grad.dtype)

        @pl.when(jnp.logical_not(kept))
        def _(grad=grad):
            grad[...] = jnp.zeros_like(grad)


def weight_grads(flags, near, far, tokens_all, cotan_all, grads, hidden, start, group):
    tokens, width = tokens_all.shape
    act_spec = pl.BlockSpec((tokens, BLK), lambda d, j, f: (0, d))
    delta_spec = pl.BlockSpec(near.shape, lambda d, j, f: (0, 0, 0))
    grad_spec = pl.BlockSpec((BLK, BLK), lambda d, j, f: (d, start + j))
    down_spec = pl.BlockSpec((BLK, BLK), lambda d, j, f: (start + j, d))
    any_spec = pl.BlockSpec(memory_space=pl.ANY)
    first = grads is None
    return pl.pallas_call(
        weight_kernel,
        grid_spec=pltpu.PrefetchScalarGridSpec(
            num_scalar_prefetch=1,
            grid=(width // BLK, group),
            in_specs=[delta_spec] * 2 + [act_spec] * 2 + ([] if first else [any_spec] * 3),
            out_specs=[grad_spec, grad_spec, down_spec],
        ),
        out_shape=[
            jax.ShapeDtypeStruct((width, hidden), jnp.bfloat16),
            jax.ShapeDtypeStruct((width, hidden), jnp.bfloat16),
            jax.ShapeDtypeStruct((hidden, width), jnp.bfloat16),
        ],
        input_output_aliases={} if first else {5: 0, 6: 1, 7: 2},
        compiler_params=pltpu.CompilerParams(vmem_limit_bytes=VMEM_LIMIT),
        cost_estimate=pl.CostEstimate(
            flops=6 * tokens * width * BLK * group,
            bytes_accessed=6 * width * BLK * group + 4 * tokens * width,
            transcendentals=0,
        ),
        name="weight_grad_part",
    )(flags, near, far, tokens_all, cotan_all, *([] if first else grads))


def swiglu(gate_value, up_value, hidden_grad):
    sigmoid = jax.nn.sigmoid(gate_value)
    swish = gate_value * sigmoid
    hidden = swish * up_value
    gate_delta = hidden_grad * up_value * sigmoid * (1.0 + gate_value * (1.0 - sigmoid))
    up_delta = hidden_grad * swish
    return jnp.stack([gate_delta, up_delta, hidden]).astype(jnp.bfloat16)


def shards(tokens, cotangent, gate_weight, up_weight, down_weight, block_mask):
    rows = lax.axis_size("row")
    levels = rows.bit_length() - 1
    row = lax.axis_index("row")
    wire = jnp.bfloat16 if rows <= 4 else jnp.float32
    hidden = gate_weight.shape[1]
    blocks = hidden // BLK
    group = 2 if blocks % 2 == 0 else 1
    groups = blocks // group

    def swap(part, bit):
        return lax.ppermute(part, "row", [(i, i ^ (1 << bit)) for i in range(rows)])

    def side(bit):
        return (row >> bit) & 1

    def after(value, earlier):
        return lax.optimization_barrier((value, earlier))

    def finish_sum(value, slope, got, order):
        give, got = after(slope[1], got)
        parts = [
            value[0] + got.astype(jnp.float32),
            slope[0] + swap(give, order[0]).astype(jnp.float32),
        ]
        for bit in order[1:]:
            half = parts[0].shape[1] // 2
            mine = [lax.dynamic_slice_in_dim(p, side(bit) * half, half, 1) for p in parts]
            other = [lax.dynamic_slice_in_dim(p, (1 - side(bit)) * half, half, 1) for p in parts]
            got = swap(jnp.concatenate([p.astype(wire) for p in other]), bit)
            parts = [
                mine[0] + got[: mine[0].shape[0]].astype(jnp.float32),
                mine[1] + got[mine[0].shape[0] :].astype(jnp.float32),
            ]
        return parts

    def spread(part, order):
        for bit in reversed(order[1:]):
            got = swap(part, bit)
            low = jnp.where(side(bit) == 0, part, got)
            high = jnp.where(side(bit) == 0, got, part)
            part = jnp.concatenate([low, high], axis=1)
        return part, swap(part, order[0])

    orders = [
        tuple(range(levels)) if g % 2 == 0 else tuple(reversed(range(levels)))
        for g in range(groups)
    ]
    flags = [
        jnp.concatenate(
            [
                side(order[0]).reshape(1).astype(jnp.int32),
                block_mask[:, :, g * group : (g + 1) * group].reshape(-1),
            ]
        )
        for g, order in enumerate(orders)
    ]

    tokens_all = lax.all_gather(tokens, "col", axis=0, tiled=True)
    cotan_all = lax.all_gather(cotangent, "col", axis=0, tiled=True)

    values, slopes, last = [], [], None
    for acts, weights, kinds, results in (
        (tokens_all, [gate_weight, up_weight], (0, 1), values),
        (cotan_all, [down_weight], (2,), slopes),
    ):
        arrived = [swap(value[1], order[0]) for value, order in zip(values, orders)]
        for g in range(groups):
            order_flags = flags[g]
            if last is not None:
                order_flags, last[0] = after(order_flags, last[0])
            if arrived and g > 0:
                order_flags, arrived[g - 1] = after(order_flags, arrived[g - 1])
            last = list(forward(order_flags, acts, weights, kinds, g * group, group, wire))
            results.append(last)
    halves = []
    for g in range(groups):
        pair, slope = finish_sum(values[g], slopes[g], arrived[g], orders[g])
        halves.append(spread(swiglu(pair[0], pair[1], slope[0]), orders[g]))
    total = jnp.zeros(tokens_all.shape, jnp.float32)
    for place in range(2):
        for g in range(groups):
            total = add_input_grad(
                flags[g],
                halves[g][place],
                place == 0,
                gate_weight,
                up_weight,
                total,
                g * group,
                group,
            )
    input_grad = lax.psum_scatter(total, "col", scatter_dimension=0, tiled=True)
    grads = None
    for g, (near, far) in enumerate(halves):
        grads = weight_grads(
            flags[g], near, far, tokens_all, cotan_all, grads, hidden, g * group, group
        )
    return (input_grad.astype(jnp.bfloat16), *grads)


def solution(mesh):
    in_specs = (
        P("col", "row"),
        P("col", "row"),
        P("row", "col"),
        P("row", "col"),
        P("col", "row"),
        P(None, "row", "col"),
    )
    out_specs = (P("col", "row"), P("row", "col"), P("row", "col"), P("col", "row"))
    return jax.shard_map(shards, mesh=mesh, in_specs=in_specs, out_specs=out_specs, check_vma=False)
```
